32 devices in a mesh: groups: 2 (over x), tx: 16 (over z, y, core).
Axes of the slice: x: 2, y: 2, z: 4, core: 2. Of those that a mesh axis runs over, the one named last changes fastest.
Arguments:
- masters: float32 [128, 1024], P(('groups', 'tx')), parts along dimension 0, may hold values from 0 to 1
- velocity: float32 [128, 1024], P(('groups', 'tx')), parts along dimension 0, may hold values from -4 to 4
- place_owner: int32 [4096, 1], P(('groups', 'tx')), parts along dimension 0, may hold values from 0 to 15; in each aligned block of 128 rows (0 to 127, 128 to 255, ...) at most 16 rows name the same one
- place_local: int32 [4096], P(('groups', 'tx')), parts along dimension 0, may hold values from 0 to 3
- place_row: int32 [4096], P(('groups', 'tx')), parts along dimension 0, may hold values from 0 to 32
- place_col: int32 [4096], P(('groups', 'tx')), parts along dimension 0, may hold values from 0 to 224
- row_taps: bfloat16 [12, 4, 2, 63], replicated, may hold values from -0.75 to 0.75
- col_taps: bfloat16 [12, 4, 2, 63], replicated, may hold values from -0.25 to 0.25
- mode_weights: float32 [12], replicated, may hold values from 0.02 to 0.2
- target: bfloat16 [2048, 256], P(('groups', 'tx')), parts along dimension 0, may hold values from 0 to 1
Outputs:
- resist_residual: float32 [2048, 256], P(('groups', 'tx')), parts along dimension 0
- velocity_new: float32 [128, 1024], P(('groups', 'tx')), parts along dimension 0
- masters_new: float32 [128, 1024], P(('groups', 'tx')), parts along dimension 0
The draws below stay inside these ranges and needn't reach their ends.
There are 2 independent parts, one for each index of `groups`. The reference program is written for one: setup_inputs(seed, part) draws one part's arguments, and reference() takes and returns one part's arrays. A program takes and returns all parts, laid end to end along the dimension named above; an argument that names none is the same for every part. Nothing has to cross between parts.
Inputs may be any that keep to these rules, and one draw needn't show every extreme that they name: `place_owner`: among the placements of one device (aligned blocks of 128), at most 16 name any one owner, a bound that some block reaches.
All inputs are finite; a program needn't handle non-finite values.
Results may differ from the reference program's by a relative error of at most 0.0012.
Values may be sent and summed in bfloat16 or wider, within the bound.
A program may use at most 192 MiB of HBM per device.

```python
import math
import jax
import jax.numpy as jnp
import numpy as np
from jax import lax

W = 256
ROW_DEV = 64
MS = 32
TAPS = 63
HALF = 31
TERMS = 4
MODES = 12
M_DEV = 4
PLC = 128
CAP = 16
NM = 64
ROWS = 1024
PLACES = 2048
N_TX = 16


def with_ends(values, stream_key, least, high):
    shape = values.shape
    index_at = [jax.random.randint(jax.random.fold_in(stream_key, axis), (), 0, shape[axis]) for axis in range(len(shape))]
    values = values.at[tuple(index_at)].set(least)
    longest = shape.index(max(shape))
    index_at[longest] = (index_at[longest] + 1) % shape[longest]
    return values.at[tuple(index_at)].set(high)


def shard_levels(own_key, extent, cuts, smallest, largest):
    def one(axis_at, parts):
        draws = jax.random.uniform(jax.random.fold_in(jax.random.fold_in(own_key, 6), axis_at), (parts,), jnp.float32, smallest / len(cuts), largest / len(cuts))
        return jnp.repeat(jnp.exp(draws), extent[axis_at] // parts).reshape((-1,) + (1,) * (len(extent) - axis_at - 1))

    level = one(*cuts[0])
    for cut in cuts[1:]:
        level = level * one(*cut)
    return level


def routed_block(key, own, number, rows, amount, top, most, lean):
    sequence = jax.random.permutation(key, amount)
    packed, common = load_shares(amount, rows * top, most, lean, True), load_shares(amount, rows * top, most, lean, False)
    places = jnp.arange(amount)

    def named(lengths, rotation):
        used = int((lengths > 0).sum())
        fixed = max(1, used // 4)
        shifted = fixed + (places - fixed + rotation * (used - fixed)) % max(1, amount - fixed)
        return jnp.zeros((amount,), jnp.int32).at[sequence[jnp.where(places < fixed, places, shifted)]].set(jnp.asarray(lengths, jnp.int32))

    lengths = jnp.where(number % 4 == 0, named(packed, number // 4), named(common, number - number // 4 - 1))
    mixed = jax.random.permutation(jax.random.fold_in(own, 3), amount)
    giver, taker = mixed[0:amount // 2 * 2:2], mixed[1:amount // 2 * 2:2]
    margin = jnp.minimum(lengths[giver] - 1, most - lengths[taker]) // 2
    margin = jnp.where((giver == sequence[0]) | (taker == sequence[0]) | (lengths[taker] == 0), 0, jnp.maximum(margin, 0))
    shifted = jax.random.randint(jax.random.fold_in(own, 4), (amount // 2,), 0, 1 << 20) % (margin + 1)
    lengths = lengths.at[giver].add(-shifted).at[taker].add(shifted)
    items = jnp.searchsorted(jnp.cumsum(lengths), jnp.arange(rows * top), side="right").astype(jnp.int32)
    table = items.reshape(top, rows).T
    table = table[jax.random.permutation(jax.random.fold_in(own, 1), rows)]
    rotation = jax.random.randint(jax.random.fold_in(own, 2), (rows, 1), 0, top)
    return jnp.take_along_axis(table, (jnp.arange(top)[None, :] + rotation) % top, axis=1)


def load_shares(count, total, limit, skew, full):
    portions = [(1 << 20) // math.isqrt(rank ** skew) + 1 for rank in range(1, count + 1)]
    largest = limit if full else min(limit, max(-(-total // count), total * portions[0] // sum(portions)))
    least = 1 if total - largest >= count - 1 else 0
    counts, spare = [largest] + [least] * (count - 1), total - largest - least * (count - 1)
    while spare > 0:
        free = [i for i in range(1, count) if counts[i] < largest] or [i for i in range(1, count) if counts[i] < limit]
        mass, budget = sum([portions[i] for i in free]), spare
        for i in free:
            more = min(limit - counts[i], max(1, budget * portions[i] // mass), spare)
            counts[i] = counts[i] + more
            spare = spare - more
    return np.array(counts)


def gaussian(key, shape, spread, limit, split=(), kind=jnp.bfloat16):
    gain = shard_levels(key, shape, split, -0.22, 0.18) if split else 1.0
    result = jax.random.normal(key, shape, jnp.float32) * spread * gain
    return jnp.minimum(jnp.maximum(result, -limit), limit).astype(kind)


def setup_inputs(seed: int = 0, part: int = 0) -> dict:
    splits = jax.random.split(jax.random.key(seed), 11)
    part_splits = jax.random.split(jax.random.fold_in(splits[10], part), 11)
    masters = jnp.clip(1.0 * jax.random.uniform(part_splits[0], (NM, MS * MS), jnp.float32) ** shard_levels(part_splits[0], (NM, MS * MS), ((0, 16),), -0.2, 0.2), 0.0, 1.0)
    velocity = gaussian(part_splits[1], (NM, MS * MS), 0.5, 4.0, ((0, 16),), jnp.float32)
    place_owner_keys = jax.random.split(jax.random.fold_in(part_splits[2], 1), PLACES // PLC)
    place_owner_turns = jax.random.permutation(jax.random.fold_in(part_splits[2], 3), PLACES // PLC)
    place_owner = jax.vmap(lambda own, number: routed_block(jax.random.fold_in(part_splits[2], 2), own, number, PLC, N_TX, 1, CAP, 2))(place_owner_keys, place_owner_turns).reshape((PLACES, 1))
    place_local = with_ends(jax.random.randint(part_splits[3], (PLACES,), 0, M_DEV), jax.random.fold_in(part_splits[3], 1), 0, M_DEV - 1).astype(jnp.int32)
    place_row = with_ends(jax.random.randint(part_splits[4], (PLACES,), 0, ROW_DEV - MS + 1), jax.random.fold_in(part_splits[4], 1), 0, ROW_DEV - MS).astype(jnp.int32)
    place_col = with_ends(jax.random.randint(part_splits[5], (PLACES,), 0, W - MS + 1), jax.random.fold_in(part_splits[5], 1), 0, W - MS).astype(jnp.int32)
    row_taps = gaussian(splits[6], (MODES, TERMS, 2, TAPS), TAPS ** -0.5, 0.75)
    col_taps = gaussian(splits[7], (MODES, TERMS, 2, TAPS), (2 * TERMS * TAPS) ** -0.5, 0.25)
    mode_weights = jnp.clip(jnp.exp(jax.random.uniform(splits[8], (MODES,), jnp.float32, math.log(0.02), math.log(0.2))), 0.02, 0.2)
    target = jnp.clip(1.0 * jax.random.uniform(part_splits[9], (ROWS, W), jnp.float32) ** shard_levels(part_splits[9], (ROWS, W), ((0, 16),), -0.2, 0.2), 0.0, 1.0).astype(jnp.bfloat16)
    return dict(masters=masters, velocity=velocity, place_owner=place_owner, place_local=place_local, place_row=place_row, place_col=place_col, row_taps=row_taps, col_taps=col_taps, mode_weights=mode_weights, target=target)


steepness = 0.5
threshold = 8.0
momentum = 0.9
step_size = 0.05


def correlate(inputs, kernel, pad_rows, pad_cols):
    return lax.conv_general_dilated(inputs, kernel, (1, 1), ((pad_rows, pad_rows), (pad_cols, pad_cols)), precision=lax.Precision.HIGHEST)


def column_kernel(col_mode):
    real_part = col_mode[:, 0].astype(jnp.float32)
    imag_part = col_mode[:, 1].astype(jnp.float32)
    to_real = jnp.stack([real_part, -imag_part], 1).reshape(2 * TERMS, TAPS)
    to_imag = jnp.stack([imag_part, real_part], 1).reshape(2 * TERMS, TAPS)
    return jnp.stack([to_real, to_imag])[:, :, None, :]


def reference(masters, velocity, place_owner, place_local, place_row, place_col, row_taps, col_taps, mode_weights, target):
    total = place_local.shape[0]
    master_id = (place_owner[:, 0] * M_DEV + place_local).astype(jnp.int32)
    master_half = masters.astype(jnp.bfloat16)
    block_index = jnp.arange(total, dtype=jnp.int32) // PLC
    first_row = (block_index * ROW_DEV + place_row).astype(jnp.int32)
    offsets = jnp.arange(MS, dtype=jnp.int32)
    flat_index = ((first_row[:, None, None] + offsets[None, :, None]) * W + place_col[:, None, None] + offsets[None, None, :]).reshape(total, MS * MS).astype(jnp.int32)
    values = master_half[master_id].astype(jnp.float32)
    canvas = jnp.zeros((ROWS * W,), jnp.float32).at[flat_index.reshape(-1)].add(values.reshape(-1))
    mask_half = lax.optimization_barrier(canvas.reshape(ROWS, W).astype(jnp.bfloat16))
    mask = mask_half.astype(jnp.float32)

    def forward_mode(pair):
        row_mode, col_mode = pair
        row_kernel = row_mode.astype(jnp.float32).reshape(2 * TERMS, 1, TAPS, 1)
        field_y = correlate(mask[None, None], row_kernel, HALF, 0)
        field_y = lax.optimization_barrier(field_y.astype(jnp.bfloat16)).astype(jnp.float32)
        return correlate(field_y, column_kernel(col_mode), 0, HALF)[0]

    fields = lax.map(forward_mode, (row_taps, col_taps))
    intensity = jnp.sum(mode_weights[:, None, None] * (fields[:, 0] ** 2 + fields[:, 1] ** 2), 0)
    resist = jax.nn.sigmoid(steepness * (intensity - threshold))
    resist_residual = resist - target.astype(jnp.float32)
    grad_intensity = resist_residual * steepness * resist * (1.0 - resist)

    def adjoint_mode(running, inputs):
        row_mode, col_mode, field, weight = inputs
        grad_field = (2.0 * weight * grad_intensity[None] * field).astype(jnp.bfloat16)
        grad_field = lax.optimization_barrier(grad_field).astype(jnp.float32)
        col_adjoint = jnp.flip(jnp.transpose(column_kernel(col_mode), (1, 0, 2, 3)), axis=3)
        grad_y = correlate(grad_field[None], col_adjoint, 0, HALF)
        grad_y = lax.optimization_barrier(grad_y.astype(jnp.bfloat16)).astype(jnp.float32)
        row_kernel = row_mode.astype(jnp.float32).reshape(2 * TERMS, 1, TAPS, 1)
        row_adjoint = jnp.flip(jnp.transpose(row_kernel, (1, 0, 2, 3)), axis=2)
        return running + correlate(grad_y, row_adjoint, HALF, 0)[0, 0], None

    grad_mask, _ = lax.scan(adjoint_mode, jnp.zeros((ROWS, W), jnp.float32), (row_taps, col_taps, fields, mode_weights))
    grad_patch = grad_mask.reshape(-1)[flat_index]
    master_grad = jax.ops.segment_sum(grad_patch, master_id, num_segments=M_DEV * N_TX)
    velocity_new = momentum * velocity + master_grad
    masters_new = masters - step_size * velocity_new
    return resist_residual, velocity_new, masters_new
```

```python
import jax
import jax.numpy as jnp
from jax import lax
from jax.experimental import pallas as pl
from jax.experimental.pallas import tpu as pltpu
from jax.sharding import PartitionSpec as P

W = 256
MS = 32
TAPS = 63
HALF = 31
TERMS = 4
MODES = 12
FILTERS = 2 * TERMS
LANES = 128


steepness = 0.5
threshold = 8.0
momentum = 0.9
step_size = 0.05


def halo(block, axis, width):
    count = lax.axis_size(axis)
    forward = [(i, i + 1) for i in range(count - 1)]
    backward = [(target, source) for source, target in forward]
    low = lax.ppermute(block[-width:], axis, forward)
    high = lax.ppermute(block[:width], axis, backward)
    return low, high


def tap_rows(row_taps, col_taps):
    row = row_taps.reshape(MODES, FILTERS, TAPS).astype(jnp.float32)
    col = col_taps.reshape(MODES, FILTERS, TAPS).astype(jnp.float32)
    rest = LANES - TAPS

    def pad(x, low, high):
        return jnp.pad(x, ((0, 0), (0, 0), (low, high)))

    row_fwd = pad(row, 0, rest)
    row_adj = jnp.concatenate([row[..., :1], pad(row[..., :0:-1], rest, 0)], axis=-1)
    col_fwd = pad(col[..., ::-1], rest, 0)
    col_adj = pad(col, rest, 0)
    return row_fwd, row_adj, col_fwd, col_adj


def rolled(taps, rows, shift):
    return pltpu.roll(
        jnp.broadcast_to(taps, (rows, LANES)), shift, 1, stride=1, stride_axis=0
    )


def column_bands(taps):
    row_iota = lax.broadcasted_iota(jnp.int32, (LANES, LANES), 0)
    lane_iota = lax.broadcasted_iota(jnp.int32, (LANES, LANES), 1)
    below = lane_iota < row_iota
    bands = []
    for c in range(FILTERS):
        circle = rolled(taps[c : c + 1], LANES, 0)
        low = jnp.where(below, circle, 0.0)
        high = jnp.where(below, 0.0, circle)
        bands.append(jnp.concatenate([low, high], axis=0))
    return bands


def filters_kernel(
    rows_here, weights_ref, row_fwd_ref, row_adj_ref, col_fwd_ref, col_adj_ref, mask_ref,
    target_ref, residual_ref, grad_ref, fields_ref,
):
    half = jnp.bfloat16
    mask = mask_ref[...]

    def forward_mode(k, intensity):
        row_taps = row_fwd_ref[k]
        row_band = jnp.concatenate(
            [rolled(row_taps[c : c + 1], rows_here, 0).astype(half) for c in range(FILTERS)], axis=0
        )
        field_y = jnp.dot(row_band, mask, preferred_element_type=jnp.float32).astype(half)
        bands = column_bands(col_fwd_ref[k])
        left, right = [], []
        for t in range(TERMS):
            re, im = bands[2 * t], bands[2 * t + 1]
            for p in range(2):
                c = 2 * t + p
                y = field_y[c * rows_here : (c + 1) * rows_here]
                left.append(jnp.concatenate([y[:, : 2 * LANES], y[:, LANES :]], axis=0))
            re_half, im_half = re.astype(half), im.astype(half)
            right.append(jnp.concatenate([re_half, im_half], axis=1))
            right.append(jnp.concatenate([(-im).astype(half), re_half], axis=1))
        field = jnp.dot(
            jnp.concatenate(left, axis=1),
            jnp.concatenate(right, axis=0),
            preferred_element_type=jnp.float32,
        )
        fields_ref[k] = field
        re, im = field[:, :LANES], field[:, LANES:]
        return intensity + weights_ref[k] * (re * re + im * im)

    intensity = lax.fori_loop(
        0, MODES, forward_mode, jnp.zeros((2 * rows_here, LANES), jnp.float32)
    )
    resist = 1.0 / (1.0 + jnp.exp(-(steepness * (intensity - threshold))))
    target = target_ref[...].astype(jnp.float32)
    target = jnp.concatenate([target[:, :LANES], target[:, LANES:]], axis=0)
    residual = resist - target
    residual_ref[:, :LANES] = residual[:rows_here]
    residual_ref[:, LANES:] = residual[rows_here:]
    grad_intensity = residual * steepness * resist * (1.0 - resist)
    grad_ref[...] = jnp.zeros(grad_ref.shape, jnp.float32)

    def adjoint_mode(k, carry):
        field = fields_ref[k]
        scale = (2.0 * weights_ref[k]) * grad_intensity
        windows = []
        for part in range(2):
            g = scale * field[:, part * LANES : (part + 1) * LANES]
            wide = jnp.concatenate(
                [g[:rows_here], g[rows_here:], jnp.zeros((rows_here, LANES), jnp.float32)], axis=1
            )
            wide = pltpu.roll(wide, 32, 1).astype(half)
            windows.append(
                jnp.concatenate([wide[:, : 2 * LANES], wide[:, LANES :]], axis=0)
            )
        bands = column_bands(col_adj_ref[k])
        right = []
        for t in range(TERMS):
            re, im = bands[2 * t], bands[2 * t + 1]
            re_half = re.astype(half)
            right.append(jnp.concatenate([re_half, im.astype(half)], axis=0))
            right.append(jnp.concatenate([(-im).astype(half), re_half], axis=0))
        grad_y = jnp.dot(
            jnp.concatenate(windows, axis=1),
            jnp.concatenate(right, axis=1),
            preferred_element_type=jnp.float32,
        ).astype(half)
        stacked = jnp.concatenate(
            [
                jnp.concatenate(
                    [
                        grad_y[:rows_here, c * LANES : (c + 1) * LANES],
                        grad_y[rows_here:, c * LANES : (c + 1) * LANES],
                    ],
                    axis=1,
                )
                for c in range(FILTERS)
            ],
            axis=0,
        )
        row_taps = row_adj_ref[k]
        first = lax.broadcasted_iota(jnp.int32, (LANES, LANES), 1) < rows_here
        row_band = jnp.concatenate(
            [
                jnp.where(
                    first,
                    rolled(row_taps[2 * t : 2 * t + 1], LANES, 0),
                    rolled(row_taps[2 * t + 1 : 2 * t + 2], LANES, rows_here),
                ).astype(half)
                for t in range(TERMS)
            ],
            axis=1,
        )
        grad_ref[...] += jnp.dot(row_band, stacked, preferred_element_type=jnp.float32)
        return carry

    lax.fori_loop(0, MODES, adjoint_mode, 0)


def run_filters(mask, target, row_taps, col_taps, mode_weights):
    rows_here = target.shape[0]
    vmem = pl.BlockSpec(memory_space=pltpu.VMEM)
    taps = tap_rows(row_taps, col_taps)

    def body(*refs):
        filters_kernel(rows_here, *refs)

    return pl.pallas_call(
        body,
        out_shape=(
            jax.ShapeDtypeStruct((rows_here, W), jnp.float32),
            jax.ShapeDtypeStruct((2 * rows_here, W), jnp.float32),
        ),
        in_specs=[pl.BlockSpec(memory_space=pltpu.SMEM)] + [vmem] * 6,
        out_specs=(vmem, vmem),
        scratch_shapes=[pltpu.VMEM((MODES, 2 * rows_here, W), jnp.float32)],
        compiler_params=pltpu.CompilerParams(vmem_limit_bytes=40 * 1024 * 1024),
        name="filters",
    )(mode_weights, *taps, mask, target)


def on_device(
    masters,
    velocity,
    place_owner,
    place_local,
    place_row,
    place_col,
    row_taps,
    col_taps,
    mode_weights,
    target,
):
    rows_here = target.shape[0]
    places = place_local.shape[0]
    devices = lax.axis_size("tx")
    master_count = masters.shape[0]
    all_masters = lax.all_gather(masters.astype(jnp.bfloat16), "tx", axis=0, tiled=True)
    master_id = place_owner[:, 0] * master_count + place_local
    offsets = jnp.arange(MS, dtype=jnp.int32)
    row_chosen = (
        place_row[:, None, None] + offsets[None, :, None]
        == jnp.arange(rows_here, dtype=jnp.int32)[None, None, :]
    )
    col_chosen = (
        place_col[:, None, None] + offsets[None, :, None]
        == jnp.arange(W, dtype=jnp.int32)[None, None, :]
    )
    chosen = (
        master_id[:, None] == jnp.arange(devices * master_count, dtype=jnp.int32)[None, :]
    )
    pattern_half = (
        jnp.dot(chosen.astype(jnp.bfloat16), all_masters, preferred_element_type=jnp.float32)
        .astype(jnp.bfloat16)
        .reshape(places, MS, MS)
    )
    spread = jnp.einsum(
        "pab,pbj->paj",
        pattern_half,
        col_chosen.astype(jnp.bfloat16),
        preferred_element_type=jnp.float32,
    ).astype(jnp.bfloat16)
    mask = jnp.einsum(
        "pai,paj->ij", row_chosen.astype(jnp.bfloat16), spread, preferred_element_type=jnp.float32
    ).astype(jnp.bfloat16)
    low, high = halo(mask, "tx", HALF)
    padded = jnp.pad(
        jnp.concatenate([low, mask, high], axis=0), ((0, 2 * rows_here - rows_here - 2 * HALF), (32, 96))
    )
    resist_residual, grad_padded = run_filters(padded, target, row_taps, col_taps, mode_weights)
    count = devices
    from_above = lax.ppermute(
        grad_padded[HALF + rows_here : 2 * HALF + rows_here],
        "tx",
        [(i, i + 1) for i in range(count - 1)],
    )
    from_below = lax.ppermute(grad_padded[:HALF], "tx", [(i + 1, i) for i in range(count - 1)])
    grad_mask = grad_padded[HALF : HALF + rows_here]
    grad_mask = grad_mask + jnp.pad(from_above, ((0, rows_here - HALF), (0, 0)))
    grad_mask = grad_mask + jnp.pad(from_below, ((rows_here - HALF, 0), (0, 0)))
    row_rows = jnp.einsum(
        "pai,ij->paj", row_chosen.astype(jnp.float32), grad_mask, precision=lax.Precision.HIGHEST
    )
    grad_patch = jnp.einsum(
        "paj,pcj->pac", row_rows, col_chosen.astype(jnp.float32), precision=lax.Precision.HIGHEST
    ).reshape(places, MS * MS)
    partial = jnp.dot(
        chosen.astype(jnp.float32).T, grad_patch, precision=lax.Precision.HIGHEST
    )
    master_grad = lax.psum_scatter(partial, "tx", scatter_dimension=0, tiled=True)
    velocity_new = momentum * velocity + master_grad
    masters_new = masters - step_size * velocity_new
    return (resist_residual, velocity_new, masters_new)


def solution(mesh):
    return jax.shard_map(
        on_device,
        mesh=mesh,
        in_specs=(
            P(("groups", "tx"), None),
            P(("groups", "tx"), None),
            P(("groups", "tx"), None),
            P(("groups", "tx")),
            P(("groups", "tx")),
            P(("groups", "tx")),
            P(),
            P(),
            P(),
            P(("groups", "tx"), None),
        ),
        out_specs=(P(("groups", "tx"), None), P(("groups", "tx"), None), P(("groups", "tx"), None)),
        check_vma=False,
    )
```

```python
import jax
import jax.numpy as jnp
from jax import lax
from jax.experimental import pallas as pl
from jax.experimental.pallas import tpu as pltpu
from jax.sharding import PartitionSpec as P

W = 256
MS = 32
TAPS = 63
HALF = 31
TERMS = 4
MODES = 12
FILTERS = 2 * TERMS
LANES = 128


steepness = 0.5
threshold = 8.0
momentum = 0.9
step_size = 0.05


def halo(block, axis, width):
    count = lax.axis_size(axis)
    forward = [(i, i + 1) for i in range(count - 1)]
    backward = [(target, source) for source, target in forward]
    low = lax.ppermute(block[-width:], axis, forward)
    high = lax.ppermute(block[:width], axis, backward)
    return low, high


def exchange(n, source, slots, send_sem, recv_sem):
    me = lax.axis_index("tx")
    barrier = pltpu.get_barrier_semaphore()

    def greet(step, carry):
        peer = lax.rem(me + step, n)
        pl.semaphore_signal(
            barrier, inc=1, device_id={"tx": peer}, device_id_type=pl.DeviceIdType.MESH
        )
        return carry

    lax.fori_loop(1, n, greet, 0)
    pl.semaphore_wait(barrier, n - 1)

    def copy(step):
        peer = lax.rem(me + step, n)
        return pltpu.make_async_remote_copy(
            src_ref=source(peer),
            dst_ref=slots.at[step],
            send_sem=send_sem.at[step],
            recv_sem=recv_sem.at[step],
            device_id={"tx": peer},
            device_id_type=pl.DeviceIdType.MESH,
        )

    def start(step, carry):
        copy(step).start()
        return carry

    def finish(step, carry):
        copy(step).wait()
        return carry

    lax.fori_loop(1, n, start, 0)
    return me, lambda: lax.fori_loop(1, n, finish, 0)


def gather_kernel(n, block_ref, out_ref, slots, send_sem, recv_sem):
    _, finish = exchange(n, lambda peer: block_ref, slots, send_sem, recv_sem)
    out_ref[0] = block_ref[...]
    finish()
    out_ref[1:] = slots[1:]


def scatter_sum_kernel(n, parts_ref, out_ref, slots, send_sem, recv_sem):
    me, finish = exchange(n, lambda peer: parts_ref.at[peer], slots, send_sem, recv_sem)
    own = parts_ref[me]
    finish()
    out_ref[...] = own + jnp.sum(slots[1:], axis=0)


def exchange_call(kernel, n, value, out_shape, collective_id, name):
    vmem = pl.BlockSpec(memory_space=pltpu.VMEM)

    def body(*refs):
        kernel(n, *refs)

    return pl.pallas_call(
        body,
        out_shape=jax.ShapeDtypeStruct(out_shape, value.dtype),
        in_specs=[vmem],
        out_specs=vmem,
        scratch_shapes=[
            pltpu.VMEM((n,) + value.shape[-2:], value.dtype),
            pltpu.SemaphoreType.DMA((n,)),
            pltpu.SemaphoreType.DMA((n,)),
        ],
        compiler_params=pltpu.CompilerParams(
            collective_id=collective_id, has_side_effects=True, vmem_limit_bytes=24 * 1024 * 1024
        ),
        name=name,
    )(value)


def tap_rows(row_taps, col_taps):
    row = row_taps.reshape(MODES, FILTERS, TAPS).astype(jnp.float32)
    col = col_taps.reshape(MODES, FILTERS, TAPS).astype(jnp.float32)
    rest = LANES - TAPS

    def pad(x, low, high):
        return jnp.pad(x, ((0, 0), (0, 0), (low, high)))

    row_fwd = pad(row, 0, rest)
    row_adj = jnp.concatenate([row[..., :1], pad(row[..., :0:-1], rest, 0)], axis=-1)
    col_fwd = pad(col[..., ::-1], rest, 0)
    col_adj = pad(col, rest, 0)
    return row_fwd, row_adj, col_fwd, col_adj


def rolled(taps, rows, shift):
    return pltpu.roll(
        jnp.broadcast_to(taps, (rows, LANES)), shift, 1, stride=1, stride_axis=0
    )


def column_bands(taps):
    row_iota = lax.broadcasted_iota(jnp.int32, (LANES, LANES), 0)
    lane_iota = lax.broadcasted_iota(jnp.int32, (LANES, LANES), 1)
    below = lane_iota < row_iota
    bands = []
    for c in range(FILTERS):
        circle = rolled(taps[c : c + 1], LANES, 0)
        low = jnp.where(below, circle, 0.0)
        high = jnp.where(below, 0.0, circle)
        bands.append(jnp.concatenate([low, high], axis=0))
    return bands


def filters_kernel(
    rows_here, weights_ref, row_fwd_ref, row_adj_ref, col_fwd_ref, col_adj_ref, mask_ref,
    target_ref, residual_ref, grad_ref, fields_ref,
):
    half = jnp.bfloat16
    mask = mask_ref[...]

    def forward_mode(k, intensity):
        row_taps = row_fwd_ref[k]
        row_band = jnp.concatenate(
            [rolled(row_taps[c : c + 1], rows_here, 0).astype(half) for c in range(FILTERS)], axis=0
        )
        field_y = jnp.dot(row_band, mask, preferred_element_type=jnp.float32).astype(half)
        bands = column_bands(col_fwd_ref[k])
        left, right = [], []
        for t in range(TERMS):
            re, im = bands[2 * t], bands[2 * t + 1]
            for p in range(2):
                c = 2 * t + p
                y = field_y[c * rows_here : (c + 1) * rows_here]
                left.append(jnp.concatenate([y[:, : 2 * LANES], y[:, LANES :]], axis=0))
            re_half, im_half = re.astype(half), im.astype(half)
            right.append(jnp.concatenate([re_half, im_half], axis=1))
            right.append(jnp.concatenate([(-im).astype(half), re_half], axis=1))
        field = jnp.dot(
            jnp.concatenate(left, axis=1),
            jnp.concatenate(right, axis=0),
            preferred_element_type=jnp.float32,
        )
        fields_ref[k] = field
        re, im = field[:, :LANES], field[:, LANES:]
        return intensity + weights_ref[k] * (re * re + im * im)

    intensity = lax.fori_loop(
        0, MODES, forward_mode, jnp.zeros((2 * rows_here, LANES), jnp.float32)
    )
    resist = 1.0 / (1.0 + jnp.exp(-(steepness * (intensity - threshold))))
    target = target_ref[...].astype(jnp.float32)
    target = jnp.concatenate([target[:, :LANES], target[:, LANES:]], axis=0)
    residual = resist - target
    residual_ref[:, :LANES] = residual[:rows_here]
    residual_ref[:, LANES:] = residual[rows_here:]
    grad_intensity = residual * steepness * resist * (1.0 - resist)
    grad_ref[...] = jnp.zeros(grad_ref.shape, jnp.float32)

    def adjoint_mode(k, carry):
        field = fields_ref[k]
        scale = (2.0 * weights_ref[k]) * grad_intensity
        windows = []
        for part in range(2):
            g = scale * field[:, part * LANES : (part + 1) * LANES]
            wide = jnp.concatenate(
                [g[:rows_here], g[rows_here:], jnp.zeros((rows_here, LANES), jnp.float32)], axis=1
            )
            wide = pltpu.roll(wide, 32, 1).astype(half)
            windows.append(
                jnp.concatenate([wide[:, : 2 * LANES], wide[:, LANES :]], axis=0)
            )
        bands = column_bands(col_adj_ref[k])
        right = []
        for t in range(TERMS):
            re, im = bands[2 * t], bands[2 * t + 1]
            re_half = re.astype(half)
            right.append(jnp.concatenate([re_half, im.astype(half)], axis=0))
            right.append(jnp.concatenate([(-im).astype(half), re_half], axis=0))
        grad_y = jnp.dot(
            jnp.concatenate(windows, axis=1),
            jnp.concatenate(right, axis=1),
            preferred_element_type=jnp.float32,
        ).astype(half)
        stacked = jnp.concatenate(
            [
                jnp.concatenate(
                    [
                        grad_y[:rows_here, c * LANES : (c + 1) * LANES],
                        grad_y[rows_here:, c * LANES : (c + 1) * LANES],
                    ],
                    axis=1,
                )
                for c in range(FILTERS)
            ],
            axis=0,
        )
        row_taps = row_adj_ref[k]
        first = lax.broadcasted_iota(jnp.int32, (LANES, LANES), 1) < rows_here
        row_band = jnp.concatenate(
            [
                jnp.where(
                    first,
                    rolled(row_taps[2 * t : 2 * t + 1], LANES, 0),
                    rolled(row_taps[2 * t + 1 : 2 * t + 2], LANES, rows_here),
                ).astype(half)
                for t in range(TERMS)
            ],
            axis=1,
        )
        grad_ref[...] += jnp.dot(row_band, stacked, preferred_element_type=jnp.float32)
        return carry

    lax.fori_loop(0, MODES, adjoint_mode, 0)


def run_filters(mask, target, row_taps, col_taps, mode_weights):
    rows_here = target.shape[0]
    vmem = pl.BlockSpec(memory_space=pltpu.VMEM)
    taps = tap_rows(row_taps, col_taps)

    def body(*refs):
        filters_kernel(rows_here, *refs)

    return pl.pallas_call(
        body,
        out_shape=(
            jax.ShapeDtypeStruct((rows_here, W), jnp.float32),
            jax.ShapeDtypeStruct((2 * rows_here, W), jnp.float32),
        ),
        in_specs=[pl.BlockSpec(memory_space=pltpu.SMEM)] + [vmem] * 6,
        out_specs=(vmem, vmem),
        scratch_shapes=[pltpu.VMEM((MODES, 2 * rows_here, W), jnp.float32)],
        compiler_params=pltpu.CompilerParams(vmem_limit_bytes=40 * 1024 * 1024),
        name="filters",
    )(mode_weights, *taps, mask, target)


def on_device(
    masters,
    velocity,
    place_owner,
    place_local,
    place_row,
    place_col,
    row_taps,
    col_taps,
    mode_weights,
    target,
):
    rows_here = target.shape[0]
    places = place_local.shape[0]
    devices = lax.axis_size("tx")
    master_count = masters.shape[0]
    tiles = master_count * MS * MS // LANES
    all_masters = exchange_call(
        gather_kernel,
        devices,
        masters.astype(jnp.bfloat16).reshape(tiles, LANES),
        (devices, tiles, LANES),
        0,
        "gather_masters",
    ).reshape(devices * master_count, MS * MS)
    master_id = place_owner[:, 0] * master_count + place_local
    distance = lax.rem(lax.axis_index("tx") - place_owner[:, 0] + devices, devices)
    slot_id = distance * master_count + place_local
    offsets = jnp.arange(MS, dtype=jnp.int32)
    row_chosen = (
        place_row[:, None, None] + offsets[None, :, None]
        == jnp.arange(rows_here, dtype=jnp.int32)[None, None, :]
    )
    col_chosen = (
        place_col[:, None, None] + offsets[None, :, None]
        == jnp.arange(W, dtype=jnp.int32)[None, None, :]
    )
    master_iota = jnp.arange(devices * master_count, dtype=jnp.int32)[None, :]
    chosen = master_id[:, None] == master_iota
    slot_chosen = slot_id[:, None] == master_iota
    pattern_half = (
        jnp.dot(slot_chosen.astype(jnp.bfloat16), all_masters, preferred_element_type=jnp.float32)
        .astype(jnp.bfloat16)
        .reshape(places, MS, MS)
    )
    spread = jnp.einsum(
        "pab,pbj->paj",
        pattern_half,
        col_chosen.astype(jnp.bfloat16),
        preferred_element_type=jnp.float32,
    ).astype(jnp.bfloat16)
    mask = jnp.einsum(
        "pai,paj->ij", row_chosen.astype(jnp.bfloat16), spread, preferred_element_type=jnp.float32
    ).astype(jnp.bfloat16)
    low, high = halo(mask, "tx", HALF)
    padded = jnp.pad(
        jnp.concatenate([low, mask, high], axis=0), ((0, 2 * rows_here - rows_here - 2 * HALF), (32, 96))
    )
    resist_residual, grad_padded = run_filters(padded, target, row_taps, col_taps, mode_weights)
    count = devices
    from_above = lax.ppermute(
        grad_padded[HALF + rows_here : 2 * HALF + rows_here],
        "tx",
        [(i, i + 1) for i in range(count - 1)],
    )
    from_below = lax.ppermute(grad_padded[:HALF], "tx", [(i + 1, i) for i in range(count - 1)])
    grad_mask = grad_padded[HALF : HALF + rows_here]
    grad_mask = grad_mask + jnp.pad(from_above, ((0, rows_here - HALF), (0, 0)))
    grad_mask = grad_mask + jnp.pad(from_below, ((rows_here - HALF, 0), (0, 0)))
    row_rows = jnp.einsum(
        "pai,ij->paj", row_chosen.astype(jnp.float32), grad_mask, precision=lax.Precision.HIGHEST
    )
    grad_patch = jnp.einsum(
        "paj,pcj->pac", row_rows, col_chosen.astype(jnp.float32), precision=lax.Precision.HIGHEST
    ).reshape(places, MS * MS)
    partial = jnp.dot(
        chosen.astype(jnp.float32).T, grad_patch, precision=lax.Precision.HIGHEST
    )
    master_grad = exchange_call(
        scatter_sum_kernel,
        devices,
        partial.reshape(devices, tiles, LANES),
        (tiles, LANES),
        1,
        "sum_gradients",
    ).reshape(master_count, MS * MS)
    velocity_new = momentum * velocity + master_grad
    masters_new = masters - step_size * velocity_new
    return (resist_residual, velocity_new, masters_new)


def solution(mesh):
    return jax.shard_map(
        on_device,
        mesh=mesh,
        in_specs=(
            P(("groups", "tx"), None),
            P(("groups", "tx"), None),
            P(("groups", "tx"), None),
            P(("groups", "tx")),
            P(("groups", "tx")),
            P(("groups", "tx")),
            P(),
            P(),
            P(),
            P(("groups", "tx"), None),
        ),
        out_specs=(P(("groups", "tx"), None), P(("groups", "tx"), None), P(("groups", "tx"), None)),
        check_vma=False,
    )
```

```python
import jax
import jax.numpy as jnp
from jax import lax
from jax.experimental import pallas as pl
from jax.experimental.pallas import tpu as pltpu
from jax.sharding import PartitionSpec as P

W = 256
MS = 32
TAPS = 63
HALF = 31
TERMS = 4
MODES = 12
FILTERS = 2 * TERMS
LANES = 128


steepness = 0.5
threshold = 8.0
momentum = 0.9
step_size = 0.05


def swap_rims(first, second, slots, send_sem, recv_sem):
    n = lax.axis_size("tx")
    me = lax.axis_index("tx")
    before, after = lax.rem(me + n - 1, n), lax.rem(me + 1, n)
    barrier = pltpu.get_barrier_semaphore()
    for peer in (before, after):
        pl.semaphore_signal(
            barrier, inc=1, device_id={"tx": peer}, device_id_type=pl.DeviceIdType.MESH
        )
    pl.semaphore_wait(barrier, 2)
    copies = [
        pltpu.make_async_remote_copy(
            src_ref=source,
            dst_ref=slots.at[slot],
            send_sem=send_sem.at[slot],
            recv_sem=recv_sem.at[slot],
            device_id={"tx": peer},
            device_id_type=pl.DeviceIdType.MESH,
        )
        for source, slot, peer in ((first, 1, before), (second, 0, after))
    ]
    for copy in copies:
        copy.start()
    for copy in copies:
        copy.wait()
    low = jnp.where(me > 0, slots[0].astype(jnp.float32), 0.0)
    high = jnp.where(me < n - 1, slots[1].astype(jnp.float32), 0.0)
    return low, high


def mask_rims_kernel(mask_ref, out_ref, slots, send_sem, recv_sem):
    rows, rim = mask_ref.shape[0], slots.shape[1]
    low, high = swap_rims(
        mask_ref.at[pl.ds(0, rim)], mask_ref.at[pl.ds(rows - rim, rim)], slots, send_sem, recv_sem
    )
    out_ref[:rim] = low.astype(out_ref.dtype)
    out_ref[rim : rim + rows] = mask_ref[...]
    out_ref[rim + rows :] = high.astype(out_ref.dtype)


def grad_rims_kernel(grad_ref, out_ref, slots, send_sem, recv_sem):
    rows, rim = out_ref.shape[0], slots.shape[1]
    low, high = swap_rims(
        grad_ref.at[pl.ds(0, rim)], grad_ref.at[pl.ds(rim + rows, rim)], slots, send_sem, recv_sem
    )
    out_ref[:rim] = grad_ref[rim : 2 * rim] + low
    out_ref[rim:] = grad_ref[2 * rim : rim + rows] + high


def rims_call(kernel, value, rows_out, collective_id, name):
    vmem = pl.BlockSpec(memory_space=pltpu.VMEM)
    return pl.pallas_call(
        kernel,
        out_shape=jax.ShapeDtypeStruct((rows_out, W), value.dtype),
        in_specs=[vmem],
        out_specs=vmem,
        scratch_shapes=[
            pltpu.VMEM((2, HALF + 1, W), value.dtype),
            pltpu.SemaphoreType.DMA((2,)),
            pltpu.SemaphoreType.DMA((2,)),
        ],
        compiler_params=pltpu.CompilerParams(collective_id=collective_id, has_side_effects=True),
        name=name,
    )(value)


def exchange(n, source, slots, send_sem, recv_sem):
    me = lax.axis_index("tx")
    barrier = pltpu.get_barrier_semaphore()

    def greet(step, carry):
        peer = lax.rem(me + step, n)
        pl.semaphore_signal(
            barrier, inc=1, device_id={"tx": peer}, device_id_type=pl.DeviceIdType.MESH
        )
        return carry

    lax.fori_loop(1, n, greet, 0)
    pl.semaphore_wait(barrier, n - 1)

    def copy(step):
        peer = lax.rem(me + step, n)
        return pltpu.make_async_remote_copy(
            src_ref=source(peer),
            dst_ref=slots.at[step],
            send_sem=send_sem.at[step],
            recv_sem=recv_sem.at[step],
            device_id={"tx": peer},
            device_id_type=pl.DeviceIdType.MESH,
        )

    def start(step, carry):
        copy(step).start()
        return carry

    def finish(step, carry):
        copy(step).wait()
        return carry

    lax.fori_loop(1, n, start, 0)
    return me, lambda: lax.fori_loop(1, n, finish, 0)


def gather_kernel(n, block_ref, out_ref, slots, send_sem, recv_sem):
    _, finish = exchange(n, lambda peer: block_ref, slots, send_sem, recv_sem)
    out_ref[0] = block_ref[...]
    finish()
    out_ref[1:] = slots[1:]


def scatter_sum_kernel(n, parts_ref, out_ref, slots, send_sem, recv_sem):
    me, finish = exchange(n, lambda peer: parts_ref.at[peer], slots, send_sem, recv_sem)
    own = parts_ref[me]
    finish()
    out_ref[...] = own + jnp.sum(slots[1:], axis=0)


def exchange_call(kernel, n, value, out_shape, collective_id, name):
    vmem = pl.BlockSpec(memory_space=pltpu.VMEM)

    def body(*refs):
        kernel(n, *refs)

    return pl.pallas_call(
        body,
        out_shape=jax.ShapeDtypeStruct(out_shape, value.dtype),
        in_specs=[vmem],
        out_specs=vmem,
        scratch_shapes=[
            pltpu.VMEM((n,) + value.shape[-2:], value.dtype),
            pltpu.SemaphoreType.DMA((n,)),
            pltpu.SemaphoreType.DMA((n,)),
        ],
        compiler_params=pltpu.CompilerParams(
            collective_id=collective_id, has_side_effects=True, vmem_limit_bytes=24 * 1024 * 1024
        ),
        name=name,
    )(value)


def tap_rows(row_taps, col_taps):
    row = row_taps.reshape(MODES, FILTERS, TAPS).astype(jnp.float32)
    col = col_taps.reshape(MODES, FILTERS, TAPS).astype(jnp.float32)
    rest = LANES - TAPS

    def pad(x, low, high):
        return jnp.pad(x, ((0, 0), (0, 0), (low, high)))

    row_fwd = pad(row, 1, rest - 1)
    row_adj = pad(row[..., ::-1], rest, 0)
    col_fwd = pad(col[..., ::-1], rest, 0)
    col_adj = pad(col, rest, 0)
    return row_fwd, row_adj, col_fwd, col_adj


def rolled(taps, rows, shift):
    return pltpu.roll(
        jnp.broadcast_to(taps, (rows, LANES)), shift, 1, stride=1, stride_axis=0
    )


def column_bands(taps):
    row_iota = lax.broadcasted_iota(jnp.int32, (LANES, LANES), 0)
    lane_iota = lax.broadcasted_iota(jnp.int32, (LANES, LANES), 1)
    below = lane_iota < row_iota
    bands = []
    for c in range(FILTERS):
        circle = rolled(taps[c : c + 1], LANES, 0)
        low = jnp.where(below, circle, 0.0)
        high = jnp.where(below, 0.0, circle)
        bands.append(jnp.concatenate([low, high], axis=0))
    return bands


def filters_kernel(
    rows_here, weights_ref, row_fwd_ref, row_adj_ref, col_fwd_ref, col_adj_ref, mask_ref,
    target_ref, residual_ref, grad_ref, fields_ref,
):
    half = jnp.bfloat16
    mask = mask_ref[...].astype(jnp.float32)
    mask = jnp.concatenate([mask, jnp.zeros((mask.shape[0], LANES), jnp.float32)], axis=1)
    mask = pltpu.roll(mask, 32, 1).astype(half)

    def forward_mode(k, intensity):
        row_taps = row_fwd_ref[k]
        row_band = jnp.concatenate(
            [rolled(row_taps[c : c + 1], rows_here, 0).astype(half) for c in range(FILTERS)], axis=0
        )
        field_y = jnp.dot(row_band, mask, preferred_element_type=jnp.float32).astype(half)
        bands = column_bands(col_fwd_ref[k])
        left, right = [], []
        for t in range(TERMS):
            re, im = bands[2 * t], bands[2 * t + 1]
            for p in range(2):
                c = 2 * t + p
                y = field_y[c * rows_here : (c + 1) * rows_here]
                left.append(jnp.concatenate([y[:, : 2 * LANES], y[:, LANES :]], axis=0))
            re_half, im_half = re.astype(half), im.astype(half)
            right.append(jnp.concatenate([re_half, im_half], axis=1))
            right.append(jnp.concatenate([(-im).astype(half), re_half], axis=1))
        field = jnp.dot(
            jnp.concatenate(left, axis=1),
            jnp.concatenate(right, axis=0),
            preferred_element_type=jnp.float32,
        )
        fields_ref[k] = field
        re, im = field[:, :LANES], field[:, LANES:]
        return intensity + weights_ref[k] * (re * re + im * im)

    intensity = lax.fori_loop(
        0, MODES, forward_mode, jnp.zeros((2 * rows_here, LANES), jnp.float32)
    )
    resist = 1.0 / (1.0 + jnp.exp(-(steepness * (intensity - threshold))))
    target = target_ref[...].astype(jnp.float32)
    target = jnp.concatenate([target[:, :LANES], target[:, LANES:]], axis=0)
    residual = resist - target
    residual_ref[:, :LANES] = residual[:rows_here]
    residual_ref[:, LANES:] = residual[rows_here:]
    grad_intensity = residual * steepness * resist * (1.0 - resist)
    grad_ref[...] = jnp.zeros(grad_ref.shape, jnp.float32)

    def adjoint_mode(k, carry):
        field = fields_ref[k]
        scale = (2.0 * weights_ref[k]) * grad_intensity
        windows = []
        for part in range(2):
            g = scale * field[:, part * LANES : (part + 1) * LANES]
            wide = jnp.concatenate(
                [g[:rows_here], g[rows_here:], jnp.zeros((rows_here, LANES), jnp.float32)], axis=1
            )
            wide = pltpu.roll(wide, 32, 1).astype(half)
            windows.append(
                jnp.concatenate([wide[:, : 2 * LANES], wide[:, LANES :]], axis=0)
            )
        bands = column_bands(col_adj_ref[k])
        right = []
        for t in range(TERMS):
            re, im = bands[2 * t], bands[2 * t + 1]
            re_half = re.astype(half)
            right.append(jnp.concatenate([re_half, im.astype(half)], axis=0))
            right.append(jnp.concatenate([(-im).astype(half), re_half], axis=0))
        grad_y = jnp.dot(
            jnp.concatenate(windows, axis=1),
            jnp.concatenate(right, axis=1),
            preferred_element_type=jnp.float32,
        ).astype(half)
        stacked = jnp.concatenate(
            [
                jnp.concatenate(
                    [
                        grad_y[:rows_here, c * LANES : (c + 1) * LANES],
                        grad_y[rows_here:, c * LANES : (c + 1) * LANES],
                    ],
                    axis=1,
                )
                for c in range(FILTERS)
            ],
            axis=0,
        )
        row_taps = row_adj_ref[k]
        first = lax.broadcasted_iota(jnp.int32, (LANES, LANES), 1) < rows_here
        row_band = jnp.concatenate(
            [
                jnp.where(
                    first,
                    rolled(row_taps[2 * t : 2 * t + 1], LANES, 0),
                    rolled(row_taps[2 * t + 1 : 2 * t + 2], LANES, rows_here),
                ).astype(half)
                for t in range(TERMS)
            ],
            axis=1,
        )
        grad_ref[...] += jnp.dot(row_band, stacked, preferred_element_type=jnp.float32)
        return carry

    lax.fori_loop(0, MODES, adjoint_mode, 0)


def run_filters(mask, target, row_taps, col_taps, mode_weights):
    rows_here = target.shape[0]
    vmem = pl.BlockSpec(memory_space=pltpu.VMEM)
    taps = tap_rows(row_taps, col_taps)

    def body(*refs):
        filters_kernel(rows_here, *refs)

    return pl.pallas_call(
        body,
        out_shape=(
            jax.ShapeDtypeStruct((rows_here, W), jnp.float32),
            jax.ShapeDtypeStruct((2 * rows_here, W), jnp.float32),
        ),
        in_specs=[pl.BlockSpec(memory_space=pltpu.SMEM)] + [vmem] * 6,
        out_specs=(vmem, vmem),
        scratch_shapes=[pltpu.VMEM((MODES, 2 * rows_here, W), jnp.float32)],
        compiler_params=pltpu.CompilerParams(vmem_limit_bytes=40 * 1024 * 1024),
        name="filters",
    )(mode_weights, *taps, mask, target)


def on_device(
    masters,
    velocity,
    place_owner,
    place_local,
    place_row,
    place_col,
    row_taps,
    col_taps,
    mode_weights,
    target,
):
    rows_here = target.shape[0]
    places = place_local.shape[0]
    devices = lax.axis_size("tx")
    master_count = masters.shape[0]
    tiles = master_count * MS * MS // LANES
    all_masters = exchange_call(
        gather_kernel,
        devices,
        masters.astype(jnp.bfloat16).reshape(tiles, LANES),
        (devices, tiles, LANES),
        0,
        "gather_masters",
    ).reshape(devices * master_count, MS * MS)
    master_id = place_owner[:, 0] * master_count + place_local
    distance = lax.rem(lax.axis_index("tx") - place_owner[:, 0] + devices, devices)
    slot_id = distance * master_count + place_local
    offsets = jnp.arange(MS, dtype=jnp.int32)
    row_chosen = (
        place_row[:, None, None] + offsets[None, :, None]
        == jnp.arange(rows_here, dtype=jnp.int32)[None, None, :]
    )
    col_chosen = (
        place_col[:, None, None] + offsets[None, :, None]
        == jnp.arange(W, dtype=jnp.int32)[None, None, :]
    )
    master_iota = jnp.arange(devices * master_count, dtype=jnp.int32)[None, :]
    chosen = master_id[:, None] == master_iota
    slot_chosen = slot_id[:, None] == master_iota
    pattern_half = (
        jnp.dot(slot_chosen.astype(jnp.bfloat16), all_masters, preferred_element_type=jnp.float32)
        .astype(jnp.bfloat16)
        .reshape(places, MS, MS)
    )
    spread = jnp.einsum(
        "pab,pbj->paj",
        pattern_half,
        col_chosen.astype(jnp.bfloat16),
        preferred_element_type=jnp.float32,
    ).astype(jnp.bfloat16)
    mask = jnp.einsum(
        "pai,paj->ij", row_chosen.astype(jnp.bfloat16), spread, preferred_element_type=jnp.float32
    ).astype(jnp.bfloat16)
    padded = rims_call(mask_rims_kernel, mask, 2 * rows_here, 2, "mask_rims")
    resist_residual, grad_padded = run_filters(padded, target, row_taps, col_taps, mode_weights)
    grad_mask = rims_call(grad_rims_kernel, grad_padded, rows_here, 3, "grad_rims")
    row_rows = jnp.einsum(
        "pai,ij->paj", row_chosen.astype(jnp.float32), grad_mask, precision=lax.Precision.HIGHEST
    )
    grad_patch = jnp.einsum(
        "paj,pcj->pac", row_rows, col_chosen.astype(jnp.float32), precision=lax.Precision.HIGHEST
    ).reshape(places, MS * MS)
    partial = jnp.dot(
        chosen.astype(jnp.float32).T, grad_patch, precision=lax.Precision.HIGHEST
    )
    master_grad = exchange_call(
        scatter_sum_kernel,
        devices,
        partial.reshape(devices, tiles, LANES),
        (tiles, LANES),
        1,
        "sum_gradients",
    ).reshape(master_count, MS * MS)
    velocity_new = momentum * velocity + master_grad
    masters_new = masters - step_size * velocity_new
    return (resist_residual, velocity_new, masters_new)


def solution(mesh):
    return jax.shard_map(
        on_device,
        mesh=mesh,
        in_specs=(
            P(("groups", "tx"), None),
            P(("groups", "tx"), None),
            P(("groups", "tx"), None),
            P(("groups", "tx")),
            P(("groups", "tx")),
            P(("groups", "tx")),
            P(),
            P(),
            P(),
            P(("groups", "tx"), None),
        ),
        out_specs=(P(("groups", "tx"), None), P(("groups", "tx"), None), P(("groups", "tx"), None)),
        check_vma=False,
    )
```

```python
import jax
import jax.numpy as jnp
from jax import lax
from jax.experimental import pallas as pl
from jax.experimental.pallas import tpu as pltpu
from jax.sharding import PartitionSpec as P

W = 256
MS = 32
TAPS = 63
HALF = 31
TERMS = 4
MODES = 12
FILTERS = 2 * TERMS
LANES = 128


steepness = 0.5
threshold = 8.0
momentum = 0.9
step_size = 0.05


def halo(block, axis, width):
    count = lax.axis_size(axis)
    forward = [(i, i + 1) for i in range(count - 1)]
    backward = [(target, source) for source, target in forward]
    low = lax.ppermute(block[-width:], axis, forward)
    high = lax.ppermute(block[:width], axis, backward)
    return low, high


def exchange(n, source, slots, send_sem, recv_sem):
    me = lax.axis_index("tx")
    barrier = pltpu.get_barrier_semaphore()

    def greet(step, carry):
        peer = lax.rem(me + step, n)
        pl.semaphore_signal(
            barrier, inc=1, device_id={"tx": peer}, device_id_type=pl.DeviceIdType.MESH
        )
        return carry

    lax.fori_loop(1, n, greet, 0)
    pl.semaphore_wait(barrier, n - 1)

    def copy(step):
        peer = lax.rem(me + step, n)
        return pltpu.make_async_remote_copy(
            src_ref=source(peer),
            dst_ref=slots.at[step],
            send_sem=send_sem.at[step],
            recv_sem=recv_sem.at[step],
            device_id={"tx": peer},
            device_id_type=pl.DeviceIdType.MESH,
        )

    def start(step, carry):
        copy(step).start()
        return carry

    def finish(step, carry):
        copy(step).wait()
        return carry

    lax.fori_loop(1, n, start, 0)
    return me, lambda: lax.fori_loop(1, n, finish, 0)


def gather_kernel(n, block_ref, out_ref, slots, send_sem, recv_sem):
    _, finish = exchange(n, lambda peer: block_ref, slots, send_sem, recv_sem)
    out_ref[0] = block_ref[...]
    finish()
    out_ref[1:] = slots[1:]


def scatter_sum_kernel(n, parts_ref, out_ref, slots, send_sem, recv_sem):
    me, finish = exchange(n, lambda peer: parts_ref.at[peer], slots, send_sem, recv_sem)
    own = parts_ref[me]
    finish()
    out_ref[...] = own + jnp.sum(slots[1:], axis=0)


def exchange_call(kernel, n, value, out_shape, collective_id, name):
    vmem = pl.BlockSpec(memory_space=pltpu.VMEM)

    def body(*refs):
        kernel(n, *refs)

    return pl.pallas_call(
        body,
        out_shape=jax.ShapeDtypeStruct(out_shape, value.dtype),
        in_specs=[vmem],
        out_specs=vmem,
        scratch_shapes=[
            pltpu.VMEM((n,) + value.shape[-2:], value.dtype),
            pltpu.SemaphoreType.DMA((n,)),
            pltpu.SemaphoreType.DMA((n,)),
        ],
        compiler_params=pltpu.CompilerParams(
            collective_id=collective_id, has_side_effects=True, vmem_limit_bytes=24 * 1024 * 1024
        ),
        name=name,
    )(value)


def tap_rows(row_taps, col_taps):
    row = row_taps.reshape(MODES, FILTERS, TAPS).astype(jnp.float32)
    col = col_taps.reshape(MODES, FILTERS, TAPS).astype(jnp.float32)
    rest = LANES - TAPS

    def pad(x, low, high):
        return jnp.pad(x, ((0, 0), (0, 0), (low, high)))

    row_fwd = pad(row, 0, rest)
    row_adj = jnp.concatenate([row[..., :1], pad(row[..., :0:-1], rest, 0)], axis=-1)
    col_fwd = pad(col[..., ::-1], rest, 0)
    col_adj = pad(col, rest, 0)
    return row_fwd, row_adj, col_fwd, col_adj


def rolled(taps, rows, shift):
    return pltpu.roll(
        jnp.broadcast_to(taps, (rows, LANES)), shift, 1, stride=1, stride_axis=0
    )


def column_bands(taps):
    row_iota = lax.broadcasted_iota(jnp.int32, (LANES, LANES), 0)
    lane_iota = lax.broadcasted_iota(jnp.int32, (LANES, LANES), 1)
    below = lane_iota < row_iota
    bands = []
    for c in range(FILTERS):
        circle = rolled(taps[c : c + 1], LANES, 0)
        low = jnp.where(below, circle, 0.0)
        high = jnp.where(below, 0.0, circle)
        bands.append(jnp.concatenate([low, high], axis=0))
    return bands


def filters_kernel(
    rows_here, weights_ref, row_fwd_ref, row_adj_ref, col_fwd_ref, col_adj_ref, mask_ref,
    target_ref, residual_ref, grad_ref, fields_ref,
):
    half = jnp.bfloat16
    mask = mask_ref[...]

    def forward_mode(k, intensity):
        row_taps = row_fwd_ref[k]
        row_band = jnp.concatenate(
            [rolled(row_taps[c : c + 1], rows_here, 0).astype(half) for c in range(FILTERS)], axis=0
        )
        field_y = jnp.dot(row_band, mask, preferred_element_type=jnp.float32).astype(half)
        bands = column_bands(col_fwd_ref[k])
        left, right = [], []
        for t in range(TERMS):
            re, im = bands[2 * t], bands[2 * t + 1]
            for p in range(2):
                c = 2 * t + p
                y = field_y[c * rows_here : (c + 1) * rows_here]
                left.append(jnp.concatenate([y[:, : 2 * LANES], y[:, LANES :]], axis=0))
            re_half, im_half = re.astype(half), im.astype(half)
            right.append(jnp.concatenate([re_half, im_half], axis=1))
            right.append(jnp.concatenate([(-im).astype(half), re_half], axis=1))
        field = jnp.dot(
            jnp.concatenate(left, axis=1),
            jnp.concatenate(right, axis=0),
            preferred_element_type=jnp.float32,
        )
        fields_ref[k] = field
        re, im = field[:, :LANES], field[:, LANES:]
        return intensity + weights_ref[k] * (re * re + im * im)

    intensity = lax.fori_loop(
        0, MODES, forward_mode, jnp.zeros((2 * rows_here, LANES), jnp.float32)
    )
    resist = 1.0 / (1.0 + jnp.exp(-(steepness * (intensity - threshold))))
    target = target_ref[...].astype(jnp.float32)
    target = jnp.concatenate([target[:, :LANES], target[:, LANES:]], axis=0)
    residual = resist - target
    residual_ref[:, :LANES] = residual[:rows_here]
    residual_ref[:, LANES:] = residual[rows_here:]
    grad_intensity = residual * steepness * resist * (1.0 - resist)
    grad_ref[...] = jnp.zeros(grad_ref.shape, jnp.float32)

    def adjoint_mode(k, carry):
        field = fields_ref[k]
        scale = (2.0 * weights_ref[k]) * grad_intensity
        windows = []
        for part in range(2):
            g = scale * field[:, part * LANES : (part + 1) * LANES]
            wide = jnp.concatenate(
                [g[:rows_here], g[rows_here:], jnp.zeros((rows_here, LANES), jnp.float32)], axis=1
            )
            wide = pltpu.roll(wide, 32, 1).astype(half)
            windows.append(
                jnp.concatenate([wide[:, : 2 * LANES], wide[:, LANES :]], axis=0)
            )
        bands = column_bands(col_adj_ref[k])
        right = []
        for t in range(TERMS):
            re, im = bands[2 * t], bands[2 * t + 1]
            re_half = re.astype(half)
            right.append(jnp.concatenate([re_half, im.astype(half)], axis=0))
            right.append(jnp.concatenate([(-im).astype(half), re_half], axis=0))
        grad_y = jnp.dot(
            jnp.concatenate(windows, axis=1),
            jnp.concatenate(right, axis=1),
            preferred_element_type=jnp.float32,
        ).astype(half)
        stacked = jnp.concatenate(
            [
                jnp.concatenate(
                    [
                        grad_y[:rows_here, c * LANES : (c + 1) * LANES],
                        grad_y[rows_here:, c * LANES : (c + 1) * LANES],
                    ],
                    axis=1,
                )
                for c in range(FILTERS)
            ],
            axis=0,
        )
        row_taps = row_adj_ref[k]
        first = lax.broadcasted_iota(jnp.int32, (LANES, LANES), 1) < rows_here
        row_band = jnp.concatenate(
            [
                jnp.where(
                    first,
                    rolled(row_taps[2 * t : 2 * t + 1], LANES, 0),
                    rolled(row_taps[2 * t + 1 : 2 * t + 2], LANES, rows_here),
                ).astype(half)
                for t in range(TERMS)
            ],
            axis=1,
        )
        grad_ref[...] += jnp.dot(row_band, stacked, preferred_element_type=jnp.float32)
        return carry

    lax.fori_loop(0, MODES, adjoint_mode, 0)


def run_filters(mask, target, row_taps, col_taps, mode_weights):
    rows_here = target.shape[0]
    vmem = pl.BlockSpec(memory_space=pltpu.VMEM)
    taps = tap_rows(row_taps, col_taps)

    def body(*refs):
        filters_kernel(rows_here, *refs)

    return pl.pallas_call(
        body,
        out_shape=(
            jax.ShapeDtypeStruct((rows_here, W), jnp.float32),
            jax.ShapeDtypeStruct((2 * rows_here, W), jnp.float32),
        ),
        in_specs=[pl.BlockSpec(memory_space=pltpu.SMEM)] + [vmem] * 6,
        out_specs=(vmem, vmem),
        scratch_shapes=[pltpu.VMEM((MODES, 2 * rows_here, W), jnp.float32)],
        compiler_params=pltpu.CompilerParams(vmem_limit_bytes=40 * 1024 * 1024),
        name="filters",
    )(mode_weights, *taps, mask, target)


def on_device(
    masters,
    velocity,
    place_owner,
    place_local,
    place_row,
    place_col,
    row_taps,
    col_taps,
    mode_weights,
    target,
):
    rows_here = target.shape[0]
    places = place_local.shape[0]
    devices = lax.axis_size("tx")
    master_count = masters.shape[0]
    tiles = master_count * MS * MS // LANES
    all_masters = exchange_call(
        gather_kernel,
        devices,
        masters.astype(jnp.bfloat16).reshape(tiles, LANES),
        (devices, tiles, LANES),
        0,
        "gather_masters",
    ).reshape(devices * master_count, MS * MS)
    master_id = place_owner[:, 0] * master_count + place_local
    distance = lax.rem(lax.axis_index("tx") - place_owner[:, 0] + devices, devices)
    slot_id = distance * master_count + place_local
    offsets = jnp.arange(MS, dtype=jnp.int32)
    row_chosen = (
        place_row[:, None, None] + offsets[None, :, None]
        == jnp.arange(rows_here, dtype=jnp.int32)[None, None, :]
    )
    col_chosen = (
        place_col[:, None, None] + offsets[None, :, None]
        == jnp.arange(W, dtype=jnp.int32)[None, None, :]
    )
    master_iota = jnp.arange(devices * master_count, dtype=jnp.int32)[None, :]
    chosen = master_id[:, None] == master_iota
    slot_chosen = slot_id[:, None] == master_iota
    pattern_half = (
        jnp.dot(slot_chosen.astype(jnp.bfloat16), all_masters, preferred_element_type=jnp.float32)
        .astype(jnp.bfloat16)
        .reshape(places, MS, MS)
    )
    spread = jnp.einsum(
        "pab,pbj->paj",
        pattern_half,
        col_chosen.astype(jnp.bfloat16),
        preferred_element_type=jnp.float32,
    ).astype(jnp.bfloat16)
    mask = jnp.einsum(
        "pai,paj->ij", row_chosen.astype(jnp.bfloat16), spread, preferred_element_type=jnp.float32
    ).astype(jnp.bfloat16)
    low, high = halo(mask, "tx", HALF)
    padded = jnp.pad(
        jnp.concatenate([low, mask, high], axis=0), ((0, 2 * rows_here - rows_here - 2 * HALF), (32, 96))
    )
    resist_residual, grad_padded = run_filters(padded, target, row_taps, col_taps, mode_weights)
    count = devices
    from_above = lax.ppermute(
        grad_padded[HALF + rows_here : 2 * HALF + rows_here],
        "tx",
        [(i, i + 1) for i in range(count - 1)],
    )
    from_below = lax.ppermute(grad_padded[:HALF], "tx", [(i + 1, i) for i in range(count - 1)])
    grad_mask = grad_padded[HALF : HALF + rows_here]
    grad_mask = grad_mask + jnp.pad(from_above, ((0, rows_here - HALF), (0, 0)))
    grad_mask = grad_mask + jnp.pad(from_below, ((rows_here - HALF, 0), (0, 0)))
    row_rows = jnp.einsum(
        "pai,ij->paj", row_chosen.astype(jnp.float32), grad_mask, precision=lax.Precision.HIGH
    )
    grad_patch = jnp.einsum(
        "paj,pcj->pac", row_rows, col_chosen.astype(jnp.float32), precision=lax.Precision.HIGH
    ).reshape(places, MS * MS)
    partial = jnp.dot(
        chosen.astype(jnp.float32).T, grad_patch, precision=lax.Precision.HIGH
    )
    master_grad = exchange_call(
        scatter_sum_kernel,
        devices,
        partial.reshape(devices, tiles, LANES),
        (tiles, LANES),
        1,
        "sum_gradients",
    ).reshape(master_count, MS * MS)
    velocity_new = momentum * velocity + master_grad
    masters_new = masters - step_size * velocity_new
    return (resist_residual, velocity_new, masters_new)


def solution(mesh):
    return jax.shard_map(
        on_device,
        mesh=mesh,
        in_specs=(
            P(("groups", "tx"), None),
            P(("groups", "tx"), None),
            P(("groups", "tx"), None),
            P(("groups", "tx")),
            P(("groups", "tx")),
            P(("groups", "tx")),
            P(),
            P(),
            P(),
            P(("groups", "tx"), None),
        ),
        out_specs=(P(("groups", "tx"), None), P(("groups", "tx"), None), P(("groups", "tx"), None)),
        check_vma=False,
    )
```

```python
import jax
import jax.numpy as jnp
from jax import lax
from jax.experimental import pallas as pl
from jax.experimental.pallas import tpu as pltpu
from jax.sharding import PartitionSpec as P

W = 256
MS = 32
TAPS = 63
HALF = 31
TERMS = 4
MODES = 12
FILTERS = 2 * TERMS
LANES = 128


steepness = 0.5
threshold = 8.0
momentum = 0.9
step_size = 0.05


def halo(block, axis, width):
    count = lax.axis_size(axis)
    forward = [(i, i + 1) for i in range(count - 1)]
    backward = [(target, source) for source, target in forward]
    low = lax.ppermute(block[-width:], axis, forward)
    high = lax.ppermute(block[:width], axis, backward)
    return low, high


def exchange(n, source, slots, send_sem, recv_sem):
    me = lax.axis_index("tx")
    barrier = pltpu.get_barrier_semaphore()

    def greet(step, carry):
        peer = lax.rem(me + step, n)
        pl.semaphore_signal(
            barrier, inc=1, device_id={"tx": peer}, device_id_type=pl.DeviceIdType.MESH
        )
        return carry

    lax.fori_loop(1, n, greet, 0)
    pl.semaphore_wait(barrier, n - 1)

    def copy(step):
        peer = lax.rem(me + step, n)
        return pltpu.make_async_remote_copy(
            src_ref=source(peer),
            dst_ref=slots.at[step],
            send_sem=send_sem.at[step],
            recv_sem=recv_sem.at[step],
            device_id={"tx": peer},
            device_id_type=pl.DeviceIdType.MESH,
        )

    def start(step, carry):
        copy(step).start()
        return carry

    def finish(step, carry):
        copy(step).wait()
        return carry

    lax.fori_loop(1, n, start, 0)
    return me, lambda: lax.fori_loop(1, n, finish, 0)


def gather_kernel(n, block_ref, out_ref, slots, send_sem, recv_sem):
    _, finish = exchange(n, lambda peer: block_ref, slots, send_sem, recv_sem)
    out_ref[0] = block_ref[...]
    finish()
    out_ref[1:] = slots[1:]


def scatter_sum_kernel(n, parts_ref, out_ref, slots, send_sem, recv_sem):
    me, finish = exchange(n, lambda peer: parts_ref.at[peer], slots, send_sem, recv_sem)
    own = parts_ref[me]
    finish()
    out_ref[...] = own + jnp.sum(slots[1:], axis=0)


def exchange_call(kernel, n, value, out_shape, collective_id, name):
    vmem = pl.BlockSpec(memory_space=pltpu.VMEM)

    def body(*refs):
        kernel(n, *refs)

    return pl.pallas_call(
        body,
        out_shape=jax.ShapeDtypeStruct(out_shape, value.dtype),
        in_specs=[vmem],
        out_specs=vmem,
        scratch_shapes=[
            pltpu.VMEM((n,) + value.shape[-2:], value.dtype),
            pltpu.SemaphoreType.DMA((n,)),
            pltpu.SemaphoreType.DMA((n,)),
        ],
        compiler_params=pltpu.CompilerParams(
            collective_id=collective_id, has_side_effects=True, vmem_limit_bytes=24 * 1024 * 1024
        ),
        name=name,
    )(value)


def tap_rows(row_taps, col_taps):
    row = row_taps.reshape(MODES, FILTERS, TAPS).astype(jnp.float32)
    col = col_taps.reshape(MODES, FILTERS, TAPS).astype(jnp.float32)
    rest = LANES - TAPS

    def pad(x, low, high):
        return jnp.pad(x, ((0, 0), (0, 0), (low, high)))

    row_fwd = pad(row, 0, rest)
    row_adj = jnp.concatenate([row[..., :1], pad(row[..., :0:-1], rest, 0)], axis=-1)
    col_fwd = pad(col[..., ::-1], rest, 0)
    col_adj = pad(col, rest, 0)
    return row_fwd, row_adj, col_fwd, col_adj


def rolled(taps, rows, shift):
    return pltpu.roll(
        jnp.broadcast_to(taps, (rows, LANES)), shift, 1, stride=1, stride_axis=0
    )


def column_bands(taps):
    row_iota = lax.broadcasted_iota(jnp.int32, (LANES, LANES), 0)
    lane_iota = lax.broadcasted_iota(jnp.int32, (LANES, LANES), 1)
    below = lane_iota < row_iota
    bands = []
    for c in range(FILTERS):
        circle = rolled(taps[c : c + 1], LANES, 0)
        low = jnp.where(below, circle, 0.0)
        high = jnp.where(below, 0.0, circle)
        bands.append(jnp.concatenate([low, high], axis=0))
    return bands


def filters_kernel(
    rows_here, weights_ref, row_fwd_ref, row_adj_ref, col_fwd_ref, col_adj_ref, mask_ref,
    target_ref, residual_ref, grad_ref, fields_ref,
):
    half = jnp.bfloat16
    mask = mask_ref[...]

    def forward_mode(k, intensity):
        row_taps = row_fwd_ref[k]
        row_band = jnp.concatenate(
            [rolled(row_taps[c : c + 1], rows_here, 0).astype(half) for c in range(FILTERS)], axis=0
        )
        field_y = jnp.dot(row_band, mask, preferred_element_type=jnp.float32).astype(half)
        bands = column_bands(col_fwd_ref[k])
        left, right = [], []
        for t in range(TERMS):
            re, im = bands[2 * t], bands[2 * t + 1]
            for p in range(2):
                c = 2 * t + p
                y = field_y[c * rows_here : (c + 1) * rows_here]
                left.append(jnp.concatenate([y[:, : 2 * LANES], y[:, LANES :]], axis=0))
            re_half, im_half = re.astype(half), im.astype(half)
            right.append(jnp.concatenate([re_half, im_half], axis=1))
            right.append(jnp.concatenate([(-im).astype(half), re_half], axis=1))
        field = jnp.dot(
            jnp.concatenate(left, axis=1),
            jnp.concatenate(right, axis=0),
            preferred_element_type=jnp.float32,
        )
        fields_ref[k] = field
        re, im = field[:, :LANES], field[:, LANES:]
        return intensity + weights_ref[k] * (re * re + im * im)

    intensity = lax.fori_loop(
        0, MODES, forward_mode, jnp.zeros((2 * rows_here, LANES), jnp.float32), unroll=2
    )
    resist = 1.0 / (1.0 + jnp.exp(-(steepness * (intensity - threshold))))
    target = target_ref[...].astype(jnp.float32)
    target = jnp.concatenate([target[:, :LANES], target[:, LANES:]], axis=0)
    residual = resist - target
    residual_ref[:, :LANES] = residual[:rows_here]
    residual_ref[:, LANES:] = residual[rows_here:]
    grad_intensity = residual * steepness * resist * (1.0 - resist)
    grad_ref[...] = jnp.zeros(grad_ref.shape, jnp.float32)

    def adjoint_mode(k, carry):
        field = fields_ref[k]
        scale = (2.0 * weights_ref[k]) * grad_intensity
        windows = []
        for part in range(2):
            g = scale * field[:, part * LANES : (part + 1) * LANES]
            wide = jnp.concatenate(
                [g[:rows_here], g[rows_here:], jnp.zeros((rows_here, LANES), jnp.float32)], axis=1
            )
            wide = pltpu.roll(wide, 32, 1).astype(half)
            windows.append(
                jnp.concatenate([wide[:, : 2 * LANES], wide[:, LANES :]], axis=0)
            )
        bands = column_bands(col_adj_ref[k])
        right = []
        for t in range(TERMS):
            re, im = bands[2 * t], bands[2 * t + 1]
            re_half = re.astype(half)
            right.append(jnp.concatenate([re_half, im.astype(half)], axis=0))
            right.append(jnp.concatenate([(-im).astype(half), re_half], axis=0))
        grad_y = jnp.dot(
            jnp.concatenate(windows, axis=1),
            jnp.concatenate(right, axis=1),
            preferred_element_type=jnp.float32,
        ).astype(half)
        stacked = jnp.concatenate(
            [
                jnp.concatenate(
                    [
                        grad_y[:rows_here, c * LANES : (c + 1) * LANES],
                        grad_y[rows_here:, c * LANES : (c + 1) * LANES],
                    ],
                    axis=1,
                )
                for c in range(FILTERS)
            ],
            axis=0,
        )
        row_taps = row_adj_ref[k]
        first = lax.broadcasted_iota(jnp.int32, (LANES, LANES), 1) < rows_here
        row_band = jnp.concatenate(
            [
                jnp.where(
                    first,
                    rolled(row_taps[2 * t : 2 * t + 1], LANES, 0),
                    rolled(row_taps[2 * t + 1 : 2 * t + 2], LANES, rows_here),
                ).astype(half)
                for t in range(TERMS)
            ],
            axis=1,
        )
        grad_ref[...] += jnp.dot(row_band, stacked, preferred_element_type=jnp.float32)
        return carry

    lax.fori_loop(0, MODES, adjoint_mode, 0, unroll=2)


def run_filters(mask, target, row_taps, col_taps, mode_weights):
    rows_here = target.shape[0]
    vmem = pl.BlockSpec(memory_space=pltpu.VMEM)
    taps = tap_rows(row_taps, col_taps)

    def body(*refs):
        filters_kernel(rows_here, *refs)

    return pl.pallas_call(
        body,
        out_shape=(
            jax.ShapeDtypeStruct((rows_here, W), jnp.float32),
            jax.ShapeDtypeStruct((2 * rows_here, W), jnp.float32),
        ),
        in_specs=[pl.BlockSpec(memory_space=pltpu.SMEM)] + [vmem] * 6,
        out_specs=(vmem, vmem),
        scratch_shapes=[pltpu.VMEM((MODES, 2 * rows_here, W), jnp.float32)],
        compiler_params=pltpu.CompilerParams(vmem_limit_bytes=40 * 1024 * 1024),
        name="filters",
    )(mode_weights, *taps, mask, target)


def on_device(
    masters,
    velocity,
    place_owner,
    place_local,
    place_row,
    place_col,
    row_taps,
    col_taps,
    mode_weights,
    target,
):
    rows_here = target.shape[0]
    places = place_local.shape[0]
    devices = lax.axis_size("tx")
    master_count = masters.shape[0]
    tiles = master_count * MS * MS // LANES
    all_masters = exchange_call(
        gather_kernel,
        devices,
        masters.astype(jnp.bfloat16).reshape(tiles, LANES),
        (devices, tiles, LANES),
        0,
        "gather_masters",
    ).reshape(devices * master_count, MS * MS)
    master_id = place_owner[:, 0] * master_count + place_local
    distance = lax.rem(lax.axis_index("tx") - place_owner[:, 0] + devices, devices)
    slot_id = distance * master_count + place_local
    offsets = jnp.arange(MS, dtype=jnp.int32)
    row_chosen = (
        place_row[:, None, None] + offsets[None, :, None]
        == jnp.arange(rows_here, dtype=jnp.int32)[None, None, :]
    )
    col_chosen = (
        place_col[:, None, None] + offsets[None, :, None]
        == jnp.arange(W, dtype=jnp.int32)[None, None, :]
    )
    master_iota = jnp.arange(devices * master_count, dtype=jnp.int32)[None, :]
    chosen = master_id[:, None] == master_iota
    slot_chosen = slot_id[:, None] == master_iota
    pattern_half = (
        jnp.dot(slot_chosen.astype(jnp.bfloat16), all_masters, preferred_element_type=jnp.float32)
        .astype(jnp.bfloat16)
        .reshape(places, MS, MS)
    )
    spread = jnp.einsum(
        "pab,pbj->paj",
        pattern_half,
        col_chosen.astype(jnp.bfloat16),
        preferred_element_type=jnp.float32,
    ).astype(jnp.bfloat16)
    mask = jnp.einsum(
        "pai,paj->ij", row_chosen.astype(jnp.bfloat16), spread, preferred_element_type=jnp.float32
    ).astype(jnp.bfloat16)
    low, high = halo(mask, "tx", HALF)
    padded = jnp.pad(
        jnp.concatenate([low, mask, high], axis=0), ((0, 2 * rows_here - rows_here - 2 * HALF), (32, 96))
    )
    resist_residual, grad_padded = run_filters(padded, target, row_taps, col_taps, mode_weights)
    count = devices
    from_above = lax.ppermute(
        grad_padded[HALF + rows_here : 2 * HALF + rows_here],
        "tx",
        [(i, i + 1) for i in range(count - 1)],
    )
    from_below = lax.ppermute(grad_padded[:HALF], "tx", [(i + 1, i) for i in range(count - 1)])
    grad_mask = grad_padded[HALF : HALF + rows_here]
    grad_mask = grad_mask + jnp.pad(from_above, ((0, rows_here - HALF), (0, 0)))
    grad_mask = grad_mask + jnp.pad(from_below, ((rows_here - HALF, 0), (0, 0)))
    row_rows = jnp.einsum(
        "pai,ij->paj", row_chosen.astype(jnp.float32), grad_mask, precision=lax.Precision.HIGH
    )
    grad_patch = jnp.einsum(
        "paj,pcj->pac", row_rows, col_chosen.astype(jnp.float32), precision=lax.Precision.HIGH
    ).reshape(places, MS * MS)
    partial = jnp.dot(
        chosen.astype(jnp.float32).T, grad_patch, precision=lax.Precision.HIGH
    )
    master_grad = exchange_call(
        scatter_sum_kernel,
        devices,
        partial.reshape(devices, tiles, LANES),
        (tiles, LANES),
        1,
        "sum_gradients",
    ).reshape(master_count, MS * MS)
    velocity_new = momentum * velocity + master_grad
    masters_new = masters - step_size * velocity_new
    return (resist_residual, velocity_new, masters_new)


def solution(mesh):
    return jax.shard_map(
        on_device,
        mesh=mesh,
        in_specs=(
            P(("groups", "tx"), None),
            P(("groups", "tx"), None),
            P(("groups", "tx"), None),
            P(("groups", "tx")),
            P(("groups", "tx")),
            P(("groups", "tx")),
            P(),
            P(),
            P(),
            P(("groups", "tx"), None),
        ),
        out_specs=(P(("groups", "tx"), None), P(("groups", "tx"), None), P(("groups", "tx"), None)),
        check_vma=False,
    )
```
